1024 devices in a mesh: fsdp: 128 (over y, z, core), grp: 8 (over x).
Axes of the slice: x: 8, y: 8, z: 8, core: 2. Of those that a mesh axis runs over, the one named last changes fastest.
Arguments:
- gradient: bfloat16 [8, 2560, 4096], P(None, 'fsdp', 'grp'), may hold values from -32 to 32
- momentum: float32 [8, 2560, 4096], P(None, 'fsdp', 'grp'), may hold values from -6 to 6
- row_counts: int32 [8, 128], replicated, may hold values from 1 to 20, 2048 in all within a row
Outputs:
- new_momentum: float32 [8, 2560, 4096], P(None, 'fsdp', 'grp')
- update: float32 [8, 2560, 4096], P(None, 'fsdp', 'grp')
The draws below stay inside these ranges and needn't reach their ends.
Inputs may be any that keep to these rules, and one draw needn't show every extreme that they name: For each matrix the counts over all owners sum to 2048; owner f holds its rows of matrix m in slots 0 to row_counts[m, f] - 1.
All inputs are finite; a program needn't handle non-finite values.
Results may differ from the reference program's by a relative error of at most 0.023.
Values may be sent and summed in bfloat16 or wider, within the bound.
A program may use at most 32 MiB of HBM per device.

```python
import math
import jax
import jax.numpy as jnp
import numpy as np
from jax import lax

D = 4096
H = 2048
MATS = 8
CAP = 20
SLOTS = 2560
N_FSDP = 128
N_GRP = 8


def draw_gradient(key, part):
    key = jax.random.fold_in(key, 11)
    noise_key, row_key, column_key = jax.random.split(key, 3)
    owner_index = (jnp.arange(SLOTS) // CAP).astype(jnp.float32)
    rising = 2.0 ** (owner_index / (N_FSDP - 1))
    row_spread = math.log(4.0)
    values = jnp.clip(jax.random.normal(noise_key, (MATS, SLOTS, D)), -5.0, 5.0)
    row_scale = rising[None, :] * jnp.exp(jax.random.uniform(row_key, (MATS, SLOTS), minval=0.0, maxval=row_spread))
    column_scale = jnp.exp(jax.random.uniform(column_key, (MATS, D), minval=0.0, maxval=math.log(3.0)))
    return (0.25 * values * row_scale[:, :, None] * column_scale[:, None, :]).astype(jnp.bfloat16)


def block_scale(rng, extent, pieces, smallest, high):
    def one(axis_at, parts):
        steps = jax.random.uniform(jax.random.fold_in(jax.random.fold_in(rng, 6), axis_at), (parts,), jnp.float32, smallest / len(pieces), high / len(pieces))
        return jnp.repeat(jnp.exp(steps), extent[axis_at] // parts).reshape((-1,) + (1,) * (len(extent) - axis_at - 1))

    loudness = one(*pieces[0])
    for cut in pieces[1:]:
        loudness = loudness * one(*cut)
    return loudness


def split_up(number_of, total, bound, slope):
    weights = [(1 << 20) // math.isqrt(standing ** slope) + 1 for standing in range(2, number_of + 1)]
    surplus, holding = total - bound - (number_of - 1), [1] * (number_of - 1)
    while surplus > 0:
        free = [i for i in range(number_of - 1) if holding[i] < bound]
        whole, budget = sum([weights[i] for i in free]), surplus
        for i in free:
            more = min(bound - holding[i], max(1, budget * weights[i] // whole), surplus)
            holding[i] = holding[i] + more
            surplus = surplus - more
    return np.array([bound] + holding)


def ragged_sizes(rng, number_of, total, most, lean):
    if number_of == 2:
        one = jax.random.randint(rng, (), max(1, total - most), min(most, total - 1) + 1)
        return jnp.stack([one, total - one])
    lengths = jnp.asarray(split_up(number_of, total, most, lean), jnp.int32)
    pairs = (number_of - 1) // 2
    giver, sink = lengths[1:1 + 2 * pairs:2], lengths[2:2 + 2 * pairs:2]
    room = jnp.minimum(giver - 1, most - sink)
    moved = jax.random.randint(jax.random.fold_in(rng, 1), (pairs,), 0, 1 << 20) % (room + 1)
    lengths = lengths.at[1:1 + 2 * pairs:2].set(giver - moved).at[2:2 + 2 * pairs:2].set(sink + moved)
    return lengths[jax.random.permutation(jax.random.fold_in(rng, 2), number_of)]


def gaussian(stream_key, dims, scale, most, pieces=(), held_as=jnp.bfloat16):
    values = jax.random.normal(stream_key, dims, jnp.float32) * scale
    if len(pieces) > 0:
        values = block_scale(stream_key, dims, pieces, -0.22, 0.18) * values
    return jnp.clip(values, min=-most, max=most).astype(held_as)


def setup_inputs(seed: int = 0) -> dict:
    streams_of = jax.random.split(jax.random.key(seed), 4)
    gradient = draw_gradient(jax.random.fold_in(streams_of[3], 71), 0)
    momentum = gaussian(streams_of[1], (MATS, SLOTS, D), 1.0, 6.0, ((1, 128), (2, 8)), jnp.float32)
    row_counts = jax.vmap(lambda own: ragged_sizes(own, N_FSDP, H, CAP, 2))(jax.random.split(streams_of[2], MATS)).reshape((MATS, N_FSDP)).astype(jnp.int32)
    return dict(gradient=gradient, momentum=momentum, row_counts=row_counts)


keep_rate = 0.95
first_coef = 1.875
third_coef = -1.25
fifth_coef = 0.375
tiny_value = 1e-06

def start_rows(row_counts):
    before = jnp.cumsum(row_counts, axis=1) - row_counts
    return before.astype(jnp.int32)

def slot_targets(starts, counts, capacity, height):
    within = jnp.arange(capacity, dtype=jnp.int32)[None, :]
    target = starts[:, None] + within
    return jnp.where(within < counts[:, None], target, height).astype(jnp.int32).reshape(-1)

def polar_step(wide_rows, gram_sum, out_scale):
    square_sum = jnp.sum(gram_sum * gram_sum)
    factor = lax.rsqrt(jnp.sqrt(square_sum / gram_sum.shape[0] + tiny_value))
    scaled = lax.optimization_barrier((gram_sum * (factor * factor)).astype(jnp.bfloat16)).astype(jnp.float32)
    first_image = jnp.dot(scaled, wide_rows, precision=lax.Precision.HIGHEST)
    first_image = lax.optimization_barrier(first_image.astype(jnp.bfloat16)).astype(jnp.float32)
    second_image = jnp.dot(scaled, first_image, precision=lax.Precision.HIGHEST)
    combined = first_coef * wide_rows + third_coef * first_image + fifth_coef * second_image
    return out_scale * factor * combined

def reference(gradient, momentum, row_counts):
    new_momentum = keep_rate * momentum + gradient.astype(jnp.float32)
    nesterov = (gradient.astype(jnp.float32) + keep_rate * new_momentum).astype(jnp.bfloat16)
    starts = start_rows(row_counts)
    block_width = D // N_GRP
    outputs = []
    for matrix_index in range(MATS):
        target = slot_targets(starts[matrix_index], row_counts[matrix_index], CAP, H)
        matrix = jnp.zeros((H, D), jnp.bfloat16).at[target].set(nesterov[matrix_index], mode='drop')
        wide_rows = matrix.astype(jnp.float32)
        gram_sum = jnp.zeros((H, H), jnp.float32)
        for block_index in range(N_GRP):
            block_cols = wide_rows[:, block_index * block_width:(block_index + 1) * block_width]
            partial_value = lax.dot_general(block_cols, block_cols, (((1,), (1,)), ((), ())), precision=lax.Precision.HIGHEST)
            gram_sum = gram_sum + lax.optimization_barrier(partial_value.astype(jnp.bfloat16)).astype(jnp.float32)
        result = polar_step(wide_rows, gram_sum, math.sqrt(D))
        clipped = jnp.minimum(target, H - 1)
        picked = jnp.take(result, clipped, axis=0)
        outputs.append(jnp.where((target < H)[:, None], picked, 0.0))
    return (new_momentum, jnp.stack(outputs))
```

```python
import math

import jax
import jax.numpy as jnp
from jax import lax
from jax.experimental import pallas as pl
from jax.experimental.pallas import tpu as pltpu
from jax.sharding import PartitionSpec as P

D = 4096
H = 2048

keep_rate = 0.95
first_coef = 1.875
third_coef = -1.25
fifth_coef = 0.375
tiny_value = 1e-06

MESH = pl.DeviceIdType.MESH
RING = 8
COLS = 512
WIDE = 640
ROWS = 160
HALF = ROWS // 2
CHUNK = 4 * ROWS
CHUNKS = 4
FULL = CHUNK * CHUNKS
PLACE = {0: 0, -1: 1, 1: 2, -2: 3, 2: 4, -3: 5, 3: 6, 4: 7}
F32 = jnp.float32
BF16 = jnp.bfloat16


def one_hot(k):
    r = lax.broadcasted_iota(jnp.int32, (32, 128), 0)
    c = lax.broadcasted_iota(jnp.int32, (32, 128), 1)
    return jnp.where(c == 16 * (r // 4) + 4 * k + r % 4, 1.0, 0.0).astype(BF16)


def one_hot_back(k):
    r = lax.broadcasted_iota(jnp.int32, (128, 32), 1)
    c = lax.broadcasted_iota(jnp.int32, (128, 32), 0)
    return jnp.where(c == 16 * (r // 4) + 4 * k + r % 4, 1.0, 0.0).astype(BF16)


def kernel(
    u_ref,
    out_ref,
    arrived,
    u_all,
    v_all,
    stage,
    got,
    got_rest,
    gram,
    w_acc,
    squares,
    reply,
    returned,
    send_sems,
    owner_sem,
    ring_u,
    sib_u,
    ring_v,
    sib_v,
    got_sem,
    rest_sem,
    spread_sem,
    square_sem,
    return_sem,
):
    f = lax.axis_index("fsdp")
    x = lax.axis_index("grp")
    y = f // 16
    z = (f // 2) % 8
    core = f % 2
    sibling = (f + 1 - 2 * core, x)

    def at_y(by):
        return (((y + by) % 8) * 16 + z * 2 + core, x)

    def at_z(by):
        return (y * 16 + ((z + by) % 8) * 2 + core, x)

    def at_x(by):
        return (f, (x + by) % 8)

    def push(src, dst, send_sem, recv_sem, device):
        pltpu.make_async_remote_copy(
            src_ref=src,
            dst_ref=dst,
            send_sem=send_sem,
            recv_sem=recv_sem,
            device_id=device,
            device_id_type=MESH,
        ).start()

    def wait(ref, sem):
        pltpu.make_async_copy(ref, ref, sem).wait()

    barrier = pltpu.get_barrier_semaphore()
    for by in range(1, 8):
        for peer in (at_y(by), at_z(by), at_x(by)):
            pl.semaphore_signal(barrier, inc=1, device_id=peer, device_id_type=MESH)
    pl.semaphore_signal(barrier, inc=1, device_id=sibling, device_id_type=MESH)
    pl.semaphore_wait(barrier, 22)

    for by in range(1, 8):
        push(u_ref.at[(y + by) % 8], arrived.at[by], send_sems.at[0], owner_sem, at_y(by))
    arrived[0] = u_ref[y]
    wait(arrived.at[pl.ds(1, 7)], owner_sem)
    for d in range(8):
        u_all[16 * d : 16 * d + 16, :] = arrived[d, :, :COLS]
    packed = arrived[:, :, COLS:].reshape(128, 128)
    for k in range(4):
        u_all[128:160, 128 * k : 128 * k + 128] = jnp.dot(
            one_hot(k), packed, preferred_element_type=F32
        ).astype(BF16)

    def gather(buf, ring_sem, sib_sem, ring_send, sib_send, on_chunk):
        def part(place, half):
            return buf.at[pl.ds(2 * ROWS * place + HALF * half, HALF)]

        def twin(place, half):
            return buf.at[pl.ds(2 * ROWS * place + ROWS + HALF * half, HALF)]

        def place_of(way, hop):
            return PLACE[4 if hop == 4 else (-hop if way == 0 else hop)]

        for half in range(2):
            for way in range(2):
                push(
                    part(0, half),
                    part(place_of(way, 1), half),
                    ring_send,
                    ring_sem.at[way, 0, half],
                    at_z(1 if way == 0 else -1),
                )
            push(part(0, half), twin(0, half), sib_send, sib_sem.at[0], sibling)
        for hop in range(1, 5):
            for half in range(2):
                for way in range(2):
                    if hop == 4 and half != way:
                        continue
                    here = place_of(way, hop)
                    wait(part(here, half), ring_sem.at[way, hop - 1, half])
                    if hop < 3 or (hop == 3 and half == way):
                        push(
                            part(here, half),
                            part(place_of(way, hop + 1), half),
                            ring_send,
                            ring_sem.at[way, hop, half],
                            at_z(1 if way == 0 else -1),
                        )
                    push(part(here, half), twin(here, half), sib_send, sib_sem.at[here], sibling)
            a = hop - 1
            for place in (2 * a, 2 * a + 1):
                wait(buf.at[pl.ds(2 * ROWS * place + ROWS, ROWS)], sib_sem.at[place])
            on_chunk(a)

    own_rows = pl.ds(pl.multiple_of(16 * x, 16), 16)

    def reduce_chunk(a):
        wait(got.at[a, pl.ds(1, 7)], got_sem.at[a])
        total = stage[a, x].astype(F32)
        for by in range(1, 8):
            total += got[a, by].astype(F32)
        gram[a, own_rows, :] = total.astype(BF16)

    def piece(kind, owner):
        if kind == 2:
            return gram.at[owner // 2, pl.ds(pl.multiple_of(128 + 16 * (owner % 2), 16), 16)]
        return gram.at[pl.ds(2 * kind, 2), pl.ds(pl.multiple_of(16 * owner, 16), 16)]

    def spread_own(kind):
        for way in range(2):
            push(
                piece(kind, x),
                piece(kind, x),
                send_sems.at[6 + kind],
                spread_sem.at[way, 0, kind],
                at_x(1 if way == 0 else -1),
            )

    def spread_hop(kind, hop):
        last_way = (0, 1, 0)[kind]
        for way in range(2):
            if hop == 4 and way != last_way:
                continue
            owner = (x - hop) % 8 if way == 0 else (x + hop) % 8
            wait(piece(kind, owner), spread_sem.at[way, hop - 1, kind])
            if hop < 3 or (hop == 3 and way == last_way):
                push(
                    piece(kind, owner),
                    piece(kind, owner),
                    send_sems.at[6 + kind],
                    spread_sem.at[way, hop, kind],
                    at_x(1 if way == 0 else -1),
                )

    def gram_chunk(a):
        product = lax.dot_general(
            u_all[0:ROWS, :],
            u_all[CHUNK * a : CHUNK * a + CHUNK, :],
            (((1,), (1,)), ((), ())),
            preferred_element_type=F32,
        )
        stage[a] = product.astype(BF16).reshape(10, 16, CHUNK)
        for by in range(1, 8):
            push(
                stage.at[a, (x + by) % 8],
                got.at[a, by],
                send_sems.at[5],
                got_sem.at[a],
                at_x(by),
            )
        if a == 2:
            reduce_chunk(0)
            reduce_chunk(1)
            spread_own(0)

    gather(u_all, ring_u, sib_u, send_sems.at[1], send_sems.at[2], gram_chunk)
    for by in range(1, 8):
        owner = (x + by) % 8
        push(
            stage.at[owner // 2, 8 + owner % 2],
            got_rest.at[by],
            send_sems.at[5],
            rest_sem,
            at_x(by),
        )
    spread_hop(0, 1)
    reduce_chunk(2)
    reduce_chunk(3)
    spread_own(1)
    wait(got_rest.at[pl.ds(1, 7)], rest_sem)
    total = stage[x // 2, 8 + x % 2].astype(F32)
    for by in range(1, 8):
        total += got_rest[by].astype(F32)
    gram[x // 2, pl.ds(pl.multiple_of(128 + 16 * (x % 2), 16), 16), :] = total.astype(BF16)
    spread_own(2)
    spread_hop(0, 2)
    spread_hop(1, 1)
    spread_hop(2, 1)
    spread_hop(0, 3)
    spread_hop(1, 2)
    spread_hop(2, 2)
    spread_hop(0, 4)
    spread_hop(1, 3)
    spread_hop(2, 3)
    spread_hop(1, 4)
    spread_hop(2, 4)

    image = jnp.zeros((ROWS, COLS), F32)
    for a in range(CHUNKS):
        image += jnp.dot(
            gram[a], u_all[CHUNK * a : CHUNK * a + CHUNK, :], preferred_element_type=F32
        )
    v_all[0:ROWS, :] = image.astype(BF16)

    def image_chunk(a):
        product = jnp.dot(
            gram[a], v_all[CHUNK * a : CHUNK * a + CHUNK, :], preferred_element_type=F32
        )
        if a == 0:
            w_acc[...] = product
        else:
            w_acc[...] += product
        if a == 0:
            sums = jnp.zeros((8, 128), F32)
            for b in range(CHUNKS):
                rows = gram[b].astype(F32)
                part = jnp.sum((rows * rows).reshape(20, 8, CHUNK), axis=0)
                for k in range(CHUNK // 128):
                    sums += part[:, 128 * k : 128 * k + 128]
            squares[0] = sums
            push(squares.at[0], squares.at[1], send_sems.at[9], square_sem.at[0], sibling)
        if a == 1:
            wait(squares.at[1], square_sem.at[0])
            squares[2] = squares[0] + squares[1]
            for by in range(1, 8):
                push(squares.at[2], squares.at[2 + by], send_sems.at[10], square_sem.at[1], at_z(by))

    gather(v_all, ring_v, sib_v, send_sems.at[3], send_sems.at[4], image_chunk)
    wait(squares.at[pl.ds(3, 7)], square_sem.at[1])
    total = squares[2]
    for by in range(1, 8):
        total += squares[2 + by]
    square_sum = jnp.sum(total, keepdims=True)
    factor = lax.rsqrt(jnp.sqrt(square_sum / H + tiny_value))
    factor_2 = factor * factor
    result = (math.sqrt(D) * factor) * (
        first_coef * u_all[0:ROWS, :].astype(F32)
        + (third_coef * factor_2) * v_all[0:ROWS, :].astype(F32)
        + (fifth_coef * factor_2 * factor_2) * w_acc[...]
    )
    result = result.astype(BF16)
    for d in range(8):
        reply[d, :, :COLS] = result[16 * d : 16 * d + 16, :]
    packed = jnp.zeros((128, 128), F32)
    for k in range(4):
        packed += jnp.dot(
            one_hot_back(k),
            result[128:160, 128 * k : 128 * k + 128],
            preferred_element_type=F32,
        )
    reply[:, :, COLS:] = packed.astype(BF16).reshape(8, 16, 128)
    for by in range(1, 8):
        push(reply.at[by], returned.at[y], send_sems.at[11], return_sem, at_y(-by))
    returned[y] = reply[0]
    wait(returned.at[pl.ds(0, 7)], return_sem)
    out_ref[...] = returned[...]

    wait(arrived.at[pl.ds(1, 7)], send_sems.at[0])
    wait(u_all.at[pl.ds(0, 7 * ROWS)], send_sems.at[1])
    wait(u_all.at[pl.ds(0, 8 * ROWS)], send_sems.at[2])
    wait(v_all.at[pl.ds(0, 7 * ROWS)], send_sems.at[3])
    wait(v_all.at[pl.ds(0, 8 * ROWS)], send_sems.at[4])
    for a in range(CHUNKS):
        wait(got.at[a, pl.ds(1, 7)], send_sems.at[5])
    wait(got_rest.at[pl.ds(1, 7)], send_sems.at[5])
    for kind in range(3):
        for _ in range(7):
            wait(piece(kind, x), send_sems.at[6 + kind])
    wait(squares.at[0], send_sems.at[9])
    wait(squares.at[pl.ds(3, 7)], send_sems.at[10])
    wait(reply.at[pl.ds(1, 7)], send_sems.at[11])


def step(packed):
    DMA = pltpu.SemaphoreType.DMA
    return pl.pallas_call(
        kernel,
        out_shape=jax.ShapeDtypeStruct((8, 16, WIDE), BF16),
        in_specs=[pl.BlockSpec(memory_space=pltpu.VMEM)],
        out_specs=pl.BlockSpec(memory_space=pltpu.VMEM),
        scratch_shapes=[
            pltpu.VMEM((8, 16, WIDE), BF16),
            pltpu.VMEM((FULL, COLS), BF16),
            pltpu.VMEM((FULL, COLS), BF16),
            pltpu.VMEM((CHUNKS, 10, 16, CHUNK), BF16),
            pltpu.VMEM((CHUNKS, 8, 16, CHUNK), BF16),
            pltpu.VMEM((8, 16, CHUNK), BF16),
            pltpu.VMEM((CHUNKS, ROWS, CHUNK), BF16),
            pltpu.VMEM((ROWS, COLS), F32),
            pltpu.VMEM((10, 8, 128), F32),
            pltpu.VMEM((8, 16, WIDE), BF16),
            pltpu.VMEM((8, 16, WIDE), BF16),
            DMA((12,)),
            DMA,
            DMA((2, 4, 2)),
            DMA((8,)),
            DMA((2, 4, 2)),
            DMA((8,)),
            DMA((CHUNKS,)),
            DMA,
            DMA((2, 4, 3)),
            DMA((2,)),
            DMA,
        ],
        compiler_params=pltpu.CompilerParams(
            collective_id=0, has_side_effects=True, vmem_limit_bytes=40 * 1024 * 1024
        ),
    )(packed)


def on_device(gradient, momentum, row_counts):
    new_momentum = keep_rate * momentum + gradient.astype(F32)
    nesterov = (gradient.astype(F32) + keep_rate * new_momentum).astype(BF16)
    matrices, capacity, columns = gradient.shape
    position = lax.axis_index("fsdp")
    counts = jnp.take(row_counts, position, axis=1)
    live = jnp.arange(capacity, dtype=jnp.int32)[None, :] < counts[:, None]
    slots = jnp.where(live[:, :, None], nesterov, jnp.zeros_like(nesterov))
    rest = slots[:, 16:, :].reshape(8, 4, 4, 128).transpose(0, 2, 1, 3).reshape(8, 16, 128)
    packed = jnp.concatenate([slots[:, :16, :], rest], axis=2)
    result = step(packed)
    rest = result[:, :, COLS:].reshape(8, 4, 4, 128).transpose(0, 2, 1, 3).reshape(8, 4, COLS)
    update = jnp.concatenate([result[:, :, :COLS], rest], axis=1).astype(F32)
    return (new_momentum, update)


def solution(mesh):
    placed = (P(None, "fsdp", "grp"), P(None, "fsdp", "grp"), P())
    return jax.shard_map(
        on_device,
        mesh=mesh,
        in_specs=placed,
        out_specs=(P(None, "fsdp", "grp"), P(None, "fsdp", "grp")),
        check_vma=False,
    )
```

```python
import math

import jax
import jax.numpy as jnp
from jax import lax
from jax.experimental import pallas as pl
from jax.experimental.pallas import tpu as pltpu
from jax.sharding import PartitionSpec as P

D = 4096
H = 2048

keep_rate = 0.95
first_coef = 1.875
third_coef = -1.25
fifth_coef = 0.375
tiny_value = 1e-06

MESH = pl.DeviceIdType.MESH
COLS = 512
WIDE = 640
ROWS = 160
CHUNK = 4 * ROWS
CHUNKS = 4
FULL = CHUNK * CHUNKS
SUBS = 5
PLACE = {0: 0, -1: 1, 1: 2, -2: 3, 2: 4, -3: 5, 3: 6, 4: 7}
ORDER = (0, 1, 7, 2, 6, 3, 5, 4)
FARTHEST_FIRST = (4, 3, 5, 2, 6, 1, 7)
F32 = jnp.float32
BF16 = jnp.bfloat16


def selection(shape, wanted):
    r = lax.broadcasted_iota(jnp.int32, shape, 0)
    c = lax.broadcasted_iota(jnp.int32, shape, 1)
    return jnp.where(c == wanted(r), 1.0, 0.0).astype(BF16)


def pick(chosen, rows):
    return jnp.dot(chosen, rows, preferred_element_type=F32)


def kernel(
    gradient_ref,
    momentum_ref,
    counts_ref,
    out_ref,
    gradient,
    momentum,
    counts,
    message,
    arrived,
    u_all,
    v_all,
    stage,
    got,
    got_rest,
    gram,
    w_acc,
    squares,
    reply,
    returned,
    local_sem,
    send_sems,
    owner_sem,
    ring_u,
    sib_u,
    ring_v,
    sib_v,
    got_sem,
    rest_sem,
    spread_sem,
    square_sem,
    return_sem,
):
    f = lax.axis_index("fsdp")
    x = lax.axis_index("grp")
    y = f // 16
    z = (f // 2) % 8
    core = f % 2
    sibling = (f + 1 - 2 * core, x)

    def at_y(by):
        return (((y + by) % 8) * 16 + z * 2 + core, x)

    def at_z(by):
        return (y * 16 + ((z + by) % 8) * 2 + core, x)

    def at_x(by):
        return (f, (x + by) % 8)

    def push(src, dst, send_sem, recv_sem, device):
        pltpu.make_async_remote_copy(
            src_ref=src,
            dst_ref=dst,
            send_sem=send_sem,
            recv_sem=recv_sem,
            device_id=device,
            device_id_type=MESH,
        ).start()

    def wait(ref, sem):
        pltpu.make_async_copy(ref, ref, sem).wait()

    barrier = pltpu.get_barrier_semaphore()
    for by in range(1, 8):
        for peer in (at_y(by), at_z(by), at_x(by)):
            pl.semaphore_signal(barrier, inc=1, device_id=peer, device_id_type=MESH)
    pl.semaphore_signal(barrier, inc=1, device_id=sibling, device_id_type=MESH)

    fetches = [
        pltpu.make_async_copy(src, dst, local_sem.at[i])
        for i, (src, dst) in enumerate(
            ((gradient_ref, gradient), (momentum_ref, momentum), (counts_ref, counts))
        )
    ]
    for fetch in fetches:
        fetch.start()
    for fetch in fetches:
        fetch.wait()
    grad = gradient[...].astype(F32)
    rows = grad + keep_rate * (keep_rate * momentum[...] + grad)
    lane = lax.broadcasted_iota(jnp.int32, (8, 128), 1)
    held = jnp.sum(jnp.where(lane == f, counts[...], 0), axis=1, keepdims=True)
    slot = lax.broadcasted_iota(jnp.int32, (20, 8, COLS), 0)
    rows = jnp.where(slot < held[None], rows, 0.0).reshape(ROWS, COLS).astype(BF16)
    main = pick(selection((128, ROWS), lambda r: 8 * (r % 16) + r // 16), rows)
    message[:, :, :COLS] = main.astype(BF16).reshape(8, 16, COLS)
    rest = jnp.zeros((128, 128), F32)
    for k in range(4):
        chosen = selection(
            (128, 32), lambda r: jnp.where(r % 16 // 4 == k, 8 * (r % 4) + r // 16, -1)
        )
        rest += pick(chosen, rows[128:ROWS, 128 * k : 128 * k + 128])
    message[:, :, COLS:] = rest.astype(BF16).reshape(8, 16, 128)

    pl.semaphore_wait(barrier, 22)

    class Ring:
        def __init__(self, buf, parts, ring_sem, sib_sem, ring_send, sib_send):
            self.buf, self.parts = buf, parts
            self.ring_sem, self.sib_sem = ring_sem, sib_sem
            self.ring_send, self.sib_send = ring_send, sib_send

        def refs(self, place, twin, sub):
            base = 2 * ROWS * place + ROWS * twin
            return [
                self.buf.at[pl.ds(start + base if isinstance(start, int) else pl.multiple_of(start + base, 16), size)]
                for start, size in self.parts[sub]
            ]

        def place(self, way, hop):
            return PLACE[4 if hop == 4 else (-hop if way == 0 else hop)]

        def forward(self, way, hop, sub):
            source = 0 if hop == 1 else self.place(way, hop - 1)
            for src, dst in zip(
                self.refs(source, 0, sub), self.refs(self.place(way, hop), 0, sub), strict=True
            ):
                push(
                    src,
                    dst,
                    self.ring_send,
                    self.ring_sem.at[way, hop - 1, sub],
                    at_z(1 if way == 0 else -1),
                )

        def twin(self, place, sub):
            for src, dst in zip(self.refs(place, 0, sub), self.refs(place, 1, sub), strict=True):
                push(src, dst, self.sib_send, self.sib_sem.at[place], sibling)

        def send_own(self, sub):
            for way in range(2):
                self.forward(way, 1, sub)
            self.twin(0, sub)

        def step(self, hop, sub):
            last_way = 0 if sub < 3 else 1
            size = sum(size for _, size in self.parts[sub])
            for way in range(2):
                if hop == 4 and way != last_way:
                    continue
                wait(self.buf.at[pl.ds(0, size)], self.ring_sem.at[way, hop - 1, sub])
                if hop < 3 or (hop == 3 and way == last_way):
                    self.forward(way, hop + 1, sub)
                self.twin(self.place(way, hop), sub)

        def settle(self, a):
            for place in (2 * a, 2 * a + 1):
                wait(self.buf.at[pl.ds(2 * ROWS * place + ROWS, ROWS)], self.sib_sem.at[place])

    group = {q: 16 * ((x + q) % 8) for q in range(-3, 5)}
    whole = Ring(
        u_all,
        [[(0, 16)], [(16, 32)], [(48, 32)], [(80, 48)], [(128, 32)]],
        ring_u,
        sib_u,
        send_sems.at[1],
        send_sems.at[2],
    )
    images = Ring(
        v_all,
        [[(group[0], 16)]]
        + [[(group[q], 16), (group[-q], 16)] for q in (1, 2, 3)]
        + [[(group[4], 16), (128, 32)]],
        ring_v,
        sib_v,
        send_sems.at[3],
        send_sems.at[4],
    )

    own_rows = pl.ds(pl.multiple_of(16 * x, 16), 16)

    def reduce_chunk(a):
        wait(got.at[a, pl.ds(1, 7)], got_sem.at[a])
        total = stage[a, x].astype(F32)
        for by in range(1, 8):
            total += got[a, by].astype(F32)
        gram[a, own_rows, :] = total.astype(BF16)

    def piece(kind, owner):
        if kind == 2:
            return gram.at[owner // 2, pl.ds(pl.multiple_of(128 + 16 * (owner % 2), 16), 16)]
        return gram.at[pl.ds(2 * kind, 2), pl.ds(pl.multiple_of(16 * owner, 16), 16)]

    def spread_own(kind):
        for way in range(2):
            push(
                piece(kind, x),
                piece(kind, x),
                send_sems.at[6 + kind],
                spread_sem.at[way, 0, kind],
                at_x(1 if way == 0 else -1),
            )

    def spread_hop(kind, hop):
        last_way = (0, 1, 0)[kind]
        for way in range(2):
            if hop == 4 and way != last_way:
                continue
            owner = (x - hop) % 8 if way == 0 else (x + hop) % 8
            wait(piece(kind, owner), spread_sem.at[way, hop - 1, kind])
            if hop < 3 or (hop == 3 and way == last_way):
                push(
                    piece(kind, owner),
                    piece(kind, owner),
                    send_sems.at[6 + kind],
                    spread_sem.at[way, hop, kind],
                    at_x(1 if way == 0 else -1),
                )

    def gram_chunk(a):
        whole.settle(a)
        product = lax.dot_general(
            u_all[0:ROWS, :],
            u_all[CHUNK * a : CHUNK * a + CHUNK, :],
            (((1,), (1,)), ((), ())),
            preferred_element_type=F32,
        )
        stage[a] = product.astype(BF16).reshape(10, 16, CHUNK)
        for by in FARTHEST_FIRST:
            push(
                stage.at[a, (x + by) % 8],
                got.at[a, by],
                send_sems.at[5],
                got_sem.at[a],
                at_x(by),
            )
        for half in range(2):
            owner = 2 * a + half

            @pl.when(x != owner)
            def _():
                push(
                    stage.at[a, 8 + half],
                    got_rest.at[(owner - x) % 8],
                    send_sems.at[5],
                    rest_sem,
                    (f, owner),
                )

    for by in FARTHEST_FIRST:
        push(message.at[(y + by) % 8], arrived.at[by], send_sems.at[0], owner_sem.at[by], at_y(by))
    arrived[0] = message[y]
    u_all[0:16, :] = arrived[0, :, :COLS]
    whole.send_own(0)

    def take(first, last):
        for p in range(first, last):
            d = ORDER[p]
            wait(arrived.at[d], owner_sem.at[d])
            u_all[16 * p : 16 * p + 16, :] = arrived[d, :, :COLS]

    take(1, 3)
    whole.send_own(1)
    take(3, 5)
    whole.send_own(2)
    take(5, 8)
    whole.send_own(3)
    packed = arrived[:, :, COLS:].reshape(128, 128)
    for k in range(4):
        chosen = selection((32, 128), lambda r: 16 * (r // 4) + 4 * k + r % 4)
        u_all[128:160, 128 * k : 128 * k + 128] = pick(chosen, packed).astype(BF16)
    whole.send_own(4)
    for hop in range(1, 5):
        for sub in range(SUBS):
            whole.step(hop, sub)
        gram_chunk(hop - 1)
        if hop == 3:
            reduce_chunk(0)
            reduce_chunk(1)
            spread_own(0)

    spread_hop(0, 1)
    reduce_chunk(2)
    reduce_chunk(3)
    spread_own(1)

    def image_of(sub):
        parts = [
            pl.ds(start if isinstance(start, int) else pl.multiple_of(start, 16), size)
            for start, size in images.parts[sub]
        ]
        total = None
        for a in range(CHUNKS):
            left = jnp.concatenate([gram[a, part, :] for part in parts], axis=0)
            product = jnp.dot(
                left, u_all[CHUNK * a : CHUNK * a + CHUNK, :], preferred_element_type=F32
            )
            total = product if total is None else total + product
        total, done = total.astype(BF16), 0
        for part in parts:
            v_all[part, :] = total[done : done + part.size]
            done += part.size
        images.send_own(sub)

    image_of(0)
    wait(got_rest.at[pl.ds(1, 7)], rest_sem)
    total = stage[x // 2, 8 + x % 2].astype(F32)
    for by in range(1, 8):
        total += got_rest[by].astype(F32)
    gram[x // 2, pl.ds(pl.multiple_of(128 + 16 * (x % 2), 16), 16), :] = total.astype(BF16)
    spread_own(2)

    def image_chunk(a):
        images.settle(a)
        product = jnp.dot(
            gram[a], v_all[CHUNK * a : CHUNK * a + CHUNK, :], preferred_element_type=F32
        )
        if a == 0:
            w_acc[...] = product
        else:
            w_acc[...] += product

    for turn in range(1, 9):
        if turn < 5:
            if turn > 1:
                spread_hop(0, turn)
            spread_hop(1, turn)
            if turn == 4:
                spread_hop(2, turn)
            image_of(turn)
            if turn < 4:
                spread_hop(2, turn)
        if turn == 4:
            sums = jnp.zeros((8, 128), F32)
            for b in range(CHUNKS):
                values = gram[b].astype(F32)
                part = jnp.sum((values * values).reshape(20, 8, CHUNK), axis=0)
                for k in range(CHUNK // 128):
                    sums += part[:, 128 * k : 128 * k + 128]
            squares[0] = sums
            push(squares.at[0], squares.at[1], send_sems.at[9], square_sem.at[0], sibling)
        if turn == 5:
            wait(squares.at[1], square_sem.at[0])
            squares[2] = squares[0] + squares[1]
            for by in range(1, 8):
                push(squares.at[2], squares.at[2 + by], send_sems.at[10], square_sem.at[1], at_z(by))
        for hop in range(1, 5):
            if 0 <= turn - hop < SUBS:
                images.step(hop, turn - hop)
        if turn >= 5:
            image_chunk(turn - 5)

    wait(squares.at[pl.ds(3, 7)], square_sem.at[1])
    total = squares[2]
    for by in range(1, 8):
        total += squares[2 + by]
    square_sum = jnp.sum(total, keepdims=True)
    factor = lax.rsqrt(jnp.sqrt(square_sum / H + tiny_value))
    factor_2 = factor * factor
    result = (math.sqrt(D) * factor) * (
        first_coef * u_all[0:ROWS, :].astype(F32)
        + (third_coef * factor_2) * v_all[0:ROWS, :].astype(F32)
        + (fifth_coef * factor_2 * factor_2) * w_acc[...]
    )
    result = result.astype(BF16)
    for p in range(8):
        reply[ORDER[p], :, :COLS] = result[16 * p : 16 * p + 16, :]
    rest = jnp.zeros((128, 128), F32)
    for k in range(4):
        chosen = selection(
            (128, 32), lambda r: jnp.where(r % 16 // 4 == k, 4 * (r // 16) + r % 4, -1)
        )
        rest += pick(chosen, result[128:160, 128 * k : 128 * k + 128])
    reply[:, :, COLS:] = rest.astype(BF16).reshape(8, 16, 128)
    for by in FARTHEST_FIRST:
        push(reply.at[by], returned.at[y], send_sems.at[11], return_sem, at_y(-by))
    returned[y] = reply[0]
    wait(returned.at[pl.ds(0, 7)], return_sem)
    main = returned[:, :, :COLS].reshape(128, COLS)
    main = pick(selection((128, 128), lambda r: 16 * (r % 8) + r // 8), main)
    out_ref[0:16] = main.reshape(16, 8, COLS).astype(BF16)
    rest = returned[:, :, COLS:].reshape(128, 128)
    for k in range(4):
        chosen = selection((32, 128), lambda r: 16 * (r % 8) + 4 * k + r // 8)
        out_ref[16:20, :, 128 * k : 128 * k + 128] = (
            pick(chosen, rest).reshape(4, 8, 128).astype(BF16)
        )

    wait(arrived.at[pl.ds(1, 7)], send_sems.at[0])
    wait(u_all.at[pl.ds(0, 7 * ROWS)], send_sems.at[1])
    wait(u_all.at[pl.ds(0, 8 * ROWS)], send_sems.at[2])
    wait(v_all.at[pl.ds(0, 7 * ROWS)], send_sems.at[3])
    wait(v_all.at[pl.ds(0, 8 * ROWS)], send_sems.at[4])
    for a in range(CHUNKS):
        wait(got.at[a, pl.ds(1, 7)], send_sems.at[5])
    wait(got_rest.at[pl.ds(1, 7)], send_sems.at[5])
    for kind in range(3):
        for _ in range(7):
            wait(piece(kind, x), send_sems.at[6 + kind])
    wait(squares.at[0], send_sems.at[9])
    wait(squares.at[pl.ds(3, 7)], send_sems.at[10])
    wait(reply.at[pl.ds(1, 7)], send_sems.at[11])


def step(gradient, momentum, row_counts):
    DMA = pltpu.SemaphoreType.DMA
    return pl.pallas_call(
        kernel,
        out_shape=jax.ShapeDtypeStruct((20, 8, COLS), BF16),
        in_specs=[pl.BlockSpec(memory_space=pl.ANY)] * 3,
        out_specs=pl.BlockSpec(memory_space=pltpu.VMEM),
        scratch_shapes=[
            pltpu.VMEM((20, 8, COLS), BF16),
            pltpu.VMEM((20, 8, COLS), F32),
            pltpu.VMEM((8, 128), jnp.int32),
            pltpu.VMEM((8, 16, WIDE), BF16),
            pltpu.VMEM((8, 16, WIDE), BF16),
            pltpu.VMEM((FULL, COLS), BF16),
            pltpu.VMEM((FULL, COLS), BF16),
            pltpu.VMEM((CHUNKS, 10, 16, CHUNK), BF16),
            pltpu.VMEM((CHUNKS, 8, 16, CHUNK), BF16),
            pltpu.VMEM((8, 16, CHUNK), BF16),
            pltpu.VMEM((CHUNKS, ROWS, CHUNK), BF16),
            pltpu.VMEM((ROWS, COLS), F32),
            pltpu.VMEM((10, 8, 128), F32),
            pltpu.VMEM((8, 16, WIDE), BF16),
            pltpu.VMEM((8, 16, WIDE), BF16),
            DMA((3,)),
            DMA((12,)),
            DMA((8,)),
            DMA((2, 4, SUBS)),
            DMA((8,)),
            DMA((2, 4, SUBS)),
            DMA((8,)),
            DMA((CHUNKS,)),
            DMA,
            DMA((2, 4, 3)),
            DMA((2,)),
            DMA,
        ],
        compiler_params=pltpu.CompilerParams(
            collective_id=0, has_side_effects=True, vmem_limit_bytes=63 * 1024 * 1024
        ),
    )(gradient, momentum, row_counts)


def on_device(gradient, momentum, row_counts):
    new_momentum = keep_rate * momentum + gradient.astype(F32)
    result = step(gradient.transpose(1, 0, 2), momentum.transpose(1, 0, 2), row_counts)
    return (new_momentum, result.transpose(1, 0, 2).astype(F32))


def solution(mesh):
    placed = (P(None, "fsdp", "grp"), P(None, "fsdp", "grp"), P())
    return jax.shard_map(
        on_device,
        mesh=mesh,
        in_specs=placed,
        out_specs=(P(None, "fsdp", "grp"), P(None, "fsdp", "grp")),
        check_vma=False,
    )
```

```python
import math

import jax
import jax.numpy as jnp
from jax import lax
from jax.experimental import pallas as pl
from jax.experimental.pallas import tpu as pltpu
from jax.sharding import PartitionSpec as P

D = 4096
H = 2048

keep_rate = 0.95
first_coef = 1.875
third_coef = -1.25
fifth_coef = 0.375
tiny_value = 1e-06

MESH = pl.DeviceIdType.MESH
COLS = 512
WIDE = 640
ROWS = 160
CHUNK = 4 * ROWS
CHUNKS = 4
FULL = CHUNK * CHUNKS
SUBS = 5
PLACE = {0: 0, -1: 1, 1: 2, -2: 3, 2: 4, -3: 5, 3: 6, 4: 7}
ORDER = (0, 1, 7, 2, 6, 3, 5, 4)
FARTHEST_FIRST = (4, 3, 5, 2, 6, 1, 7)
NEAREST_FIRST = (1, 7, 2, 6, 3, 5, 4)
SHORT_U = ()
SHORT_V = (3, 4)
SHORT_X = (2, 3)
LAST_WAY_X = (0, 1, 1, 0)
F32 = jnp.float32
BF16 = jnp.bfloat16


def selection(shape, wanted):
    r = lax.broadcasted_iota(jnp.int32, shape, 0)
    c = lax.broadcasted_iota(jnp.int32, shape, 1)
    return jnp.where(c == wanted(r), 1.0, 0.0).astype(BF16)


def pick(chosen, rows):
    return jnp.dot(chosen, rows, preferred_element_type=F32)


def kernel(
    gradient_ref,
    momentum_ref,
    counts_ref,
    out_ref,
    gradient,
    momentum,
    counts,
    message,
    arrived,
    u_all,
    v_all,
    stage,
    got,
    got_rest,
    gram,
    w_acc,
    squares,
    reply,
    returned,
    local_sem,
    send_sems,
    owner_sem,
    ring_u,
    sib_u,
    ring_v,
    sib_v,
    got_sem,
    rest_sem,
    spread_sem,
    square_sem,
    return_sem,
):
    f = lax.axis_index("fsdp")
    x = lax.axis_index("grp")
    y = f // 16
    z = (f // 2) % 8
    core = f % 2
    sibling = (f + 1 - 2 * core, x)

    def at_y(by):
        return (((y + by) % 8) * 16 + z * 2 + core, x)

    def at_z(by):
        return (y * 16 + ((z + by) % 8) * 2 + core, x)

    def at_x(by):
        return (f, (x + by) % 8)

    def push(src, dst, send_sem, recv_sem, device):
        pltpu.make_async_remote_copy(
            src_ref=src,
            dst_ref=dst,
            send_sem=send_sem,
            recv_sem=recv_sem,
            device_id=device,
            device_id_type=MESH,
        ).start()

    def wait(ref, sem):
        pltpu.make_async_copy(ref, ref, sem).wait()

    fetches = [
        pltpu.make_async_copy(src, dst, local_sem.at[i])
        for i, (src, dst) in enumerate(
            ((gradient_ref, gradient), (momentum_ref, momentum), (counts_ref, counts))
        )
    ]
    for fetch in fetches:
        fetch.start()

    barrier = pltpu.get_barrier_semaphore()
    for by in range(1, 8):
        for peer in (at_y(by), at_z(by), at_x(by)):
            pl.semaphore_signal(barrier, inc=1, device_id=peer, device_id_type=MESH)
    pl.semaphore_signal(barrier, inc=1, device_id=sibling, device_id_type=MESH)

    for fetch in fetches:
        fetch.wait()
    grad = gradient[...].astype(F32)
    rows = grad + keep_rate * (keep_rate * momentum[...] + grad)
    lane = lax.broadcasted_iota(jnp.int32, (8, 128), 1)
    held = jnp.sum(jnp.where(lane == f, counts[...], 0), axis=1, keepdims=True)
    slot = lax.broadcasted_iota(jnp.int32, (20, 8, COLS), 0)
    rows = jnp.where(slot < held[None], rows, 0.0).reshape(ROWS, COLS).astype(BF16)
    main = pick(selection((128, ROWS), lambda r: 8 * (r % 16) + r // 16), rows)
    message[:, :, :COLS] = main.astype(BF16).reshape(8, 16, COLS)
    rest = jnp.zeros((128, 128), F32)
    for k in range(4):
        chosen = selection(
            (128, 32), lambda r: jnp.where(r % 16 // 4 == k, 8 * (r % 4) + r // 16, -1)
        )
        rest += pick(chosen, rows[128:ROWS, 128 * k : 128 * k + 128])
    message[:, :, COLS:] = rest.astype(BF16).reshape(8, 16, 128)

    pl.semaphore_wait(barrier, 22)

    class Ring:
        def __init__(self, buf, parts, short, ring_sem, sib_sem, ring_send, sib_send):
            self.short = short
            self.buf, self.parts = buf, parts
            self.ring_sem, self.sib_sem = ring_sem, sib_sem
            self.ring_send, self.sib_send = ring_send, sib_send

        def refs(self, place, twin, sub):
            base = 2 * ROWS * place + ROWS * twin
            return [
                self.buf.at[pl.ds(start + base if isinstance(start, int) else pl.multiple_of(start + base, 16), size)]
                for start, size in self.parts[sub]
            ]

        def place(self, way, hop):
            return PLACE[4 if hop == 4 else (-hop if way == 0 else hop)]

        def forward(self, way, hop, sub, chips=1):
            source = 0 if hop == chips else self.place(way, hop - chips)
            for src, dst in zip(
                self.refs(source, 0, sub), self.refs(self.place(way, hop), 0, sub), strict=True
            ):
                push(
                    src,
                    dst,
                    self.ring_send,
                    self.ring_sem.at[way, hop - 1, sub],
                    at_z(chips if way == 0 else -chips),
                )

        def twin(self, place, sub):
            for src, dst in zip(self.refs(place, 0, sub), self.refs(place, 1, sub), strict=True):
                push(src, dst, self.sib_send, self.sib_sem.at[place], sibling)

        def send_own(self, sub):
            for way in range(2):
                if sub in self.short:
                    self.forward(way, 2, sub, 2)
                self.forward(way, 1, sub)
            self.twin(0, sub)

        def step(self, hop, sub):
            last_way = 0 if sub < 3 else 1
            size = sum(size for _, size in self.parts[sub])
            for way in range(2):
                if hop == 4 and way != last_way:
                    continue
                wait(self.buf.at[pl.ds(0, size)], self.ring_sem.at[way, hop - 1, sub])
                if sub in self.short:
                    if hop == 2:
                        if way == last_way:
                            self.forward(way, 4, sub, 2)
                        self.forward(way, 3, sub)
                elif hop < 3 or (hop == 3 and way == last_way):
                    self.forward(way, hop + 1, sub)
                self.twin(self.place(way, hop), sub)

        def settle(self, a):
            for place in (2 * a, 2 * a + 1):
                wait(self.buf.at[pl.ds(2 * ROWS * place + ROWS, ROWS)], self.sib_sem.at[place])

    group = {q: 16 * ((x + q) % 8) for q in range(-3, 5)}
    whole = Ring(
        u_all,
        [[(0, 16)], [(16, 32)], [(48, 32)], [(80, 48)], [(128, 32)]],
        SHORT_U,
        ring_u,
        sib_u,
        send_sems.at[1],
        send_sems.at[2],
    )
    images = Ring(
        v_all,
        [[(group[0], 16)]]
        + [[(group[q], 16), (group[-q], 16)] for q in (1, 2, 3)]
        + [[(group[4], 16), (128, 32)]],
        SHORT_V,
        ring_v,
        sib_v,
        send_sems.at[3],
        send_sems.at[4],
    )

    own_rows = pl.ds(pl.multiple_of(16 * x, 16), 16)

    def reduce_chunk(a):
        wait(got.at[a, pl.ds(1, 7)], got_sem.at[a])
        total = stage[a, x].astype(F32)
        for by in range(1, 8):
            total += got[a, by].astype(F32)
        gram[a, own_rows, :] = total.astype(BF16)

    def piece(kind, owner):
        if kind == 3:
            return gram.at[owner // 2, pl.ds(pl.multiple_of(128 + 16 * (owner % 2), 16), 16)]
        first, chunks = ((0, 2), (2, 1), (3, 1))[kind]
        return gram.at[pl.ds(first, chunks), pl.ds(pl.multiple_of(16 * owner, 16), 16)]

    def spread(kind, way, hop, chips=1):
        far = hop - chips
        owner = (x - far) % 8 if way == 0 else (x + far) % 8
        push(
            piece(kind, owner),
            piece(kind, owner),
            send_sems.at[6 + kind],
            spread_sem.at[way, hop - 1, kind],
            at_x(chips if way == 0 else -chips),
        )

    def spread_own(kind):
        for way in range(2):
            if kind in SHORT_X:
                spread(kind, way, 2, 2)
            spread(kind, way, 1)

    def spread_hop(kind, hop):
        last_way = LAST_WAY_X[kind]
        for way in range(2):
            if hop == 4 and way != last_way:
                continue
            owner = (x - hop) % 8 if way == 0 else (x + hop) % 8
            wait(piece(kind, owner), spread_sem.at[way, hop - 1, kind])
            if kind in SHORT_X:
                if hop == 2:
                    if way == last_way:
                        spread(kind, way, 4, 2)
                    spread(kind, way, 3)
            elif hop < 3 or (hop == 3 and way == last_way):
                spread(kind, way, hop + 1)

    def gram_chunk(a):
        whole.settle(a)
        product = lax.dot_general(
            u_all[0:ROWS, :],
            u_all[CHUNK * a : CHUNK * a + CHUNK, :],
            (((1,), (1,)), ((), ())),
            preferred_element_type=F32,
        )
        stage[a] = product.astype(BF16).reshape(10, 16, CHUNK)
        for by in FARTHEST_FIRST:
            push(
                stage.at[a, (x + by) % 8],
                got.at[a, by],
                send_sems.at[5],
                got_sem.at[a],
                at_x(by),
            )
        for half in range(2):
            owner = 2 * a + half

            @pl.when(x != owner)
            def _():
                push(
                    stage.at[a, 8 + half],
                    got_rest.at[(owner - x) % 8],
                    send_sems.at[5],
                    rest_sem,
                    (f, owner),
                )

    for by in NEAREST_FIRST:
        push(message.at[(y + by) % 8], arrived.at[by], send_sems.at[0], owner_sem.at[by], at_y(by))
    arrived[0] = message[y]
    u_all[0:16, :] = arrived[0, :, :COLS]
    whole.send_own(0)

    def take(first, last):
        for p in range(first, last):
            d = ORDER[p]
            wait(arrived.at[d], owner_sem.at[d])
            u_all[16 * p : 16 * p + 16, :] = arrived[d, :, :COLS]

    take(1, 3)
    whole.send_own(1)
    take(3, 5)
    whole.send_own(2)
    take(5, 8)
    whole.send_own(3)
    packed = arrived[:, :, COLS:].reshape(128, 128)
    for k in range(4):
        chosen = selection((32, 128), lambda r: 16 * (r // 4) + 4 * k + r % 4)
        u_all[128:160, 128 * k : 128 * k + 128] = pick(chosen, packed).astype(BF16)
    whole.send_own(4)
    for hop in range(1, 5):
        for sub in range(SUBS):
            whole.step(hop, sub)
        gram_chunk(hop - 1)
        if hop == 3:
            reduce_chunk(0)
            reduce_chunk(1)
            spread_own(0)

    spread_hop(0, 1)
    reduce_chunk(2)
    spread_own(1)
    spread_hop(0, 2)
    reduce_chunk(3)
    spread_own(2)

    def image_of(sub):
        parts = [
            pl.ds(start if isinstance(start, int) else pl.multiple_of(start, 16), size)
            for start, size in images.parts[sub]
        ]
        total = None
        for a in range(CHUNKS):
            left = jnp.concatenate([gram[a, part, :] for part in parts], axis=0)
            product = jnp.dot(
                left, u_all[CHUNK * a : CHUNK * a + CHUNK, :], preferred_element_type=F32
            )
            total = product if total is None else total + product
        total, done = total.astype(BF16), 0
        for part in parts:
            v_all[part, :] = total[done : done + part.size]
            done += part.size
        images.send_own(sub)

    wait(got_rest.at[pl.ds(1, 7)], rest_sem)
    total = stage[x // 2, 8 + x % 2].astype(F32)
    for by in range(1, 8):
        total += got_rest[by].astype(F32)
    gram[x // 2, pl.ds(pl.multiple_of(128 + 16 * (x % 2), 16), 16), :] = total.astype(BF16)
    spread_own(3)
    image_of(0)

    def image_chunk(a):
        images.settle(a)
        product = jnp.dot(
            gram[a], v_all[CHUNK * a : CHUNK * a + CHUNK, :], preferred_element_type=F32
        )
        if a == 0:
            w_acc[...] = product
        else:
            w_acc[...] += product

    for turn in range(1, 9):
        if turn < 5:
            spread_hop(1, turn)
            spread_hop(2, turn)
            if turn in (2, 4):
                spread_hop(3, turn)
            image_of(turn)
            if turn in (1, 3):
                spread_hop(3, turn)
            if turn < 3:
                spread_hop(0, turn + 2)
        if turn == 4:
            sums = jnp.zeros((8, 128), F32)
            for b in range(CHUNKS):
                values = gram[b].astype(F32)
                part = jnp.sum((values * values).reshape(20, 8, CHUNK), axis=0)
                for k in range(CHUNK // 128):
                    sums += part[:, 128 * k : 128 * k + 128]
            squares[0] = sums
            push(squares.at[0], squares.at[1], send_sems.at[10], square_sem.at[0], sibling)
        if turn == 5:
            wait(squares.at[1], square_sem.at[0])
            squares[2] = squares[0] + squares[1]
            for by in range(1, 8):
                push(squares.at[2], squares.at[2 + by], send_sems.at[11], square_sem.at[1], at_z(by))
        for hop in range(1, 5):
            if 0 <= turn - hop < SUBS:
                images.step(hop, turn - hop)
        if turn >= 5:
            image_chunk(turn - 5)

    wait(squares.at[pl.ds(3, 7)], square_sem.at[1])
    total = squares[2]
    for by in range(1, 8):
        total += squares[2 + by]
    square_sum = jnp.sum(total, keepdims=True)
    factor = lax.rsqrt(jnp.sqrt(square_sum / H + tiny_value))
    factor_2 = factor * factor
    result = (math.sqrt(D) * factor) * (
        first_coef * u_all[0:ROWS, :].astype(F32)
        + (third_coef * factor_2) * v_all[0:ROWS, :].astype(F32)
        + (fifth_coef * factor_2 * factor_2) * w_acc[...]
    )
    result = result.astype(BF16)
    for p in range(8):
        reply[ORDER[p], :, :COLS] = result[16 * p : 16 * p + 16, :]
    rest = jnp.zeros((128, 128), F32)
    for k in range(4):
        chosen = selection(
            (128, 32), lambda r: jnp.where(r % 16 // 4 == k, 4 * (r // 16) + r % 4, -1)
        )
        rest += pick(chosen, result[128:160, 128 * k : 128 * k + 128])
    reply[:, :, COLS:] = rest.astype(BF16).reshape(8, 16, 128)
    for by in FARTHEST_FIRST:
        push(reply.at[by], returned.at[y], send_sems.at[12], return_sem, at_y(-by))
    returned[y] = reply[0]
    wait(returned.at[pl.ds(0, 7)], return_sem)
    main = returned[:, :, :COLS].reshape(128, COLS)
    main = pick(selection((128, 128), lambda r: 16 * (r % 8) + r // 8), main)
    out_ref[0:16] = main.reshape(16, 8, COLS).astype(BF16)
    rest = returned[:, :, COLS:].reshape(128, 128)
    for k in range(4):
        chosen = selection((32, 128), lambda r: 16 * (r % 8) + 4 * k + r // 8)
        out_ref[16:20, :, 128 * k : 128 * k + 128] = (
            pick(chosen, rest).reshape(4, 8, 128).astype(BF16)
        )

    wait(arrived.at[pl.ds(1, 7)], send_sems.at[0])
    wait(u_all.at[pl.ds(0, 7 * ROWS)], send_sems.at[1])
    wait(u_all.at[pl.ds(0, 8 * ROWS)], send_sems.at[2])
    wait(v_all.at[pl.ds(0, 7 * ROWS)], send_sems.at[3])
    wait(v_all.at[pl.ds(0, 8 * ROWS)], send_sems.at[4])
    for a in range(CHUNKS):
        wait(got.at[a, pl.ds(1, 7)], send_sems.at[5])
    wait(got_rest.at[pl.ds(1, 7)], send_sems.at[5])
    for kind in range(4):
        for _ in range(7):
            wait(piece(kind, x), send_sems.at[6 + kind])
    wait(squares.at[0], send_sems.at[10])
    wait(squares.at[pl.ds(3, 7)], send_sems.at[11])
    wait(reply.at[pl.ds(1, 7)], send_sems.at[12])


def step(gradient, momentum, row_counts):
    DMA = pltpu.SemaphoreType.DMA
    return pl.pallas_call(
        kernel,
        out_shape=jax.ShapeDtypeStruct((20, 8, COLS), BF16),
        in_specs=[pl.BlockSpec(memory_space=pl.ANY)] * 3,
        out_specs=pl.BlockSpec(memory_space=pltpu.VMEM),
        scratch_shapes=[
            pltpu.VMEM((20, 8, COLS), BF16),
            pltpu.VMEM((20, 8, COLS), F32),
            pltpu.VMEM((8, 128), jnp.int32),
            pltpu.VMEM((8, 16, WIDE), BF16),
            pltpu.VMEM((8, 16, WIDE), BF16),
            pltpu.VMEM((FULL, COLS), BF16),
            pltpu.VMEM((FULL, COLS), BF16),
            pltpu.VMEM((CHUNKS, 10, 16, CHUNK), BF16),
            pltpu.VMEM((CHUNKS, 8, 16, CHUNK), BF16),
            pltpu.VMEM((8, 16, CHUNK), BF16),
            pltpu.VMEM((CHUNKS, ROWS, CHUNK), BF16),
            pltpu.VMEM((ROWS, COLS), F32),
            pltpu.VMEM((10, 8, 128), F32),
            pltpu.VMEM((8, 16, WIDE), BF16),
            pltpu.VMEM((8, 16, WIDE), BF16),
            DMA((3,)),
            DMA((13,)),
            DMA((8,)),
            DMA((2, 4, SUBS)),
            DMA((8,)),
            DMA((2, 4, SUBS)),
            DMA((8,)),
            DMA((CHUNKS,)),
            DMA,
            DMA((2, 4, 4)),
            DMA((2,)),
            DMA,
        ],
        compiler_params=pltpu.CompilerParams(
            collective_id=0, has_side_effects=True, vmem_limit_bytes=63 * 1024 * 1024
        ),
    )(gradient, momentum, row_counts)


def on_device(gradient, momentum, row_counts):
    new_momentum = keep_rate * momentum + gradient.astype(F32)
    result = step(gradient.transpose(1, 0, 2), momentum.transpose(1, 0, 2), row_counts)
    return (new_momentum, result.transpose(1, 0, 2).astype(F32))


def solution(mesh):
    placed = (P(None, "fsdp", "grp"), P(None, "fsdp", "grp"), P())
    return jax.shard_map(
        on_device,
        mesh=mesh,
        in_specs=placed,
        out_specs=(P(None, "fsdp", "grp"), P(None, "fsdp", "grp")),
        check_vma=False,
    )
```

```python
import math

import jax
import jax.numpy as jnp
from jax import lax
from jax.experimental import pallas as pl
from jax.experimental.pallas import tpu as pltpu
from jax.sharding import PartitionSpec as P

D = 4096
H = 2048

keep_rate = 0.95
first_coef = 1.875
third_coef = -1.25
fifth_coef = 0.375
tiny_value = 1e-06

MESH = pl.DeviceIdType.MESH
COLS = 512
WIDE = 640
ROWS = 160
CHUNK = 4 * ROWS
CHUNKS = 4
FULL = CHUNK * CHUNKS
SUBS = 5
PLACE = {0: 0, -1: 1, 1: 2, -2: 3, 2: 4, -3: 5, 3: 6, 4: 7}
ORDER = (0, 1, 7, 2, 6, 3, 5, 4)
FARTHEST_FIRST = (4, 3, 5, 2, 6, 1, 7)
NEAREST_FIRST = (1, 7, 2, 6, 3, 5, 4)
SHORT_U = ()
SHORT_V = (3, 4)
SHORT_X = (2, 3)
LAST_WAY_X = (0, 1, 1, 0)
F32 = jnp.float32
BF16 = jnp.bfloat16


def selection(shape, wanted):
    r = lax.broadcasted_iota(jnp.int32, shape, 0)
    c = lax.broadcasted_iota(jnp.int32, shape, 1)
    return jnp.where(c == wanted(r), 1.0, 0.0).astype(BF16)


def pick(chosen, rows):
    return jnp.dot(chosen, rows, preferred_element_type=F32)


def kernel(
    gradient_ref,
    momentum_ref,
    counts_ref,
    out_ref,
    gradient,
    momentum,
    counts,
    message,
    arrived,
    u_all,
    v_all,
    stage,
    got,
    got_rest,
    gram,
    w_acc,
    squares,
    reply,
    returned,
    local_sem,
    send_sems,
    owner_sem,
    ring_u,
    sib_u,
    ring_v,
    sib_v,
    got_sem,
    rest_sem,
    spread_sem,
    square_sem,
    return_sem,
):
    f = lax.axis_index("fsdp")
    x = lax.axis_index("grp")
    y = f // 16
    z = (f // 2) % 8
    core = f % 2
    sibling = (f + 1 - 2 * core, x)

    def at_y(by):
        return (((y + by) % 8) * 16 + z * 2 + core, x)

    def at_z(by):
        return (y * 16 + ((z + by) % 8) * 2 + core, x)

    def at_x(by):
        return (f, (x + by) % 8)

    def push(src, dst, send_sem, recv_sem, device):
        pltpu.make_async_remote_copy(
            src_ref=src,
            dst_ref=dst,
            send_sem=send_sem,
            recv_sem=recv_sem,
            device_id=device,
            device_id_type=MESH,
        ).start()

    def wait(ref, sem):
        pltpu.make_async_copy(ref, ref, sem).wait()

    fetches = [
        pltpu.make_async_copy(src, dst, local_sem.at[i])
        for i, (src, dst) in enumerate(
            ((gradient_ref, gradient), (momentum_ref, momentum), (counts_ref, counts))
        )
    ]
    for fetch in fetches:
        fetch.start()

    barrier = pltpu.get_barrier_semaphore()
    for by in range(1, 8):
        for peer in (at_y(by), at_z(by), at_x(by)):
            pl.semaphore_signal(barrier, inc=1, device_id=peer, device_id_type=MESH)
    pl.semaphore_signal(barrier, inc=1, device_id=sibling, device_id_type=MESH)

    for fetch in fetches:
        fetch.wait()
    grad = gradient[...].astype(F32)
    rows = grad + keep_rate * (keep_rate * momentum[...] + grad)
    lane = lax.broadcasted_iota(jnp.int32, (8, 128), 1)
    held = jnp.sum(jnp.where(lane == f, counts[...], 0), axis=1, keepdims=True)
    slot = lax.broadcasted_iota(jnp.int32, (20, 8, COLS), 0)
    rows = jnp.where(slot < held[None], rows, 0.0).reshape(ROWS, COLS).astype(BF16)
    main = pick(selection((128, ROWS), lambda r: 8 * (r % 16) + r // 16), rows)
    message[:, :, :COLS] = main.astype(BF16).reshape(8, 16, COLS)
    rest = jnp.zeros((128, 128), F32)
    for k in range(4):
        chosen = selection(
            (128, 32), lambda r: jnp.where(r % 16 // 4 == k, 8 * (r % 4) + r // 16, -1)
        )
        rest += pick(chosen, rows[128:ROWS, 128 * k : 128 * k + 128])
    message[:, :, COLS:] = rest.astype(BF16).reshape(8, 16, 128)

    pl.semaphore_wait(barrier, 22)

    class Ring:
        def __init__(self, buf, parts, short, ring_sem, sib_sem, ring_send, sib_send):
            self.short = short
            self.buf, self.parts = buf, parts
            self.ring_sem, self.sib_sem = ring_sem, sib_sem
            self.ring_send, self.sib_send = ring_send, sib_send

        def refs(self, place, twin, sub):
            base = 2 * ROWS * place + ROWS * twin
            return [
                self.buf.at[pl.ds(start + base if isinstance(start, int) else pl.multiple_of(start + base, 16), size)]
                for start, size in self.parts[sub]
            ]

        def place(self, way, hop):
            return PLACE[4 if hop == 4 else (-hop if way == 0 else hop)]

        def forward(self, way, hop, sub, chips=1):
            source = 0 if hop == chips else self.place(way, hop - chips)
            for src, dst in zip(
                self.refs(source, 0, sub), self.refs(self.place(way, hop), 0, sub), strict=True
            ):
                push(
                    src,
                    dst,
                    self.ring_send,
                    self.ring_sem.at[way, hop - 1, sub],
                    at_z(chips if way == 0 else -chips),
                )

        def twin(self, place, sub):
            for src, dst in zip(self.refs(place, 0, sub), self.refs(place, 1, sub), strict=True):
                push(src, dst, self.sib_send, self.sib_sem.at[place], sibling)

        def send_own(self, sub):
            for way in range(2):
                if sub in self.short:
                    self.forward(way, 2, sub, 2)
                self.forward(way, 1, sub)
            self.twin(0, sub)

        def step(self, hop, sub):
            last_way = 0 if sub < 3 else 1
            size = sum(size for _, size in self.parts[sub])
            for way in range(2):
                if hop == 4 and way != last_way:
                    continue
                wait(self.buf.at[pl.ds(0, size)], self.ring_sem.at[way, hop - 1, sub])
                if sub in self.short:
                    if hop == 2:
                        if way == last_way:
                            self.forward(way, 4, sub, 2)
                        self.forward(way, 3, sub)
                elif hop < 3 or (hop == 3 and way == last_way):
                    self.forward(way, hop + 1, sub)
                self.twin(self.place(way, hop), sub)

        def settle(self, a):
            for place in (2 * a, 2 * a + 1):
                wait(self.buf.at[pl.ds(2 * ROWS * place + ROWS, ROWS)], self.sib_sem.at[place])

    group = {q: 16 * ((x + q) % 8) for q in range(-3, 5)}
    whole = Ring(
        u_all,
        [[(0, 16)], [(16, 32)], [(48, 32)], [(80, 48)], [(128, 32)]],
        SHORT_U,
        ring_u,
        sib_u,
        send_sems.at[1],
        send_sems.at[2],
    )
    images = Ring(
        v_all,
        [[(group[0], 16)]]
        + [[(group[q], 16), (group[-q], 16)] for q in (1, 2, 3)]
        + [[(group[4], 16), (128, 32)]],
        SHORT_V,
        ring_v,
        sib_v,
        send_sems.at[3],
        send_sems.at[4],
    )

    own_rows = pl.ds(pl.multiple_of(16 * x, 16), 16)

    def reduce_chunk(a):
        wait(got.at[a, pl.ds(1, 7)], got_sem.at[a])
        total = stage[a, x].astype(F32)
        for by in range(1, 8):
            total += got[a, by].astype(F32)
        gram[a, own_rows, :] = total.astype(BF16)

    def piece(kind, owner):
        if kind == 3:
            return gram.at[owner // 2, pl.ds(pl.multiple_of(128 + 16 * (owner % 2), 16), 16)]
        first, chunks = ((0, 2), (2, 1), (3, 1))[kind]
        return gram.at[pl.ds(first, chunks), pl.ds(pl.multiple_of(16 * owner, 16), 16)]

    def spread(kind, way, hop, chips=1):
        far = hop - chips
        owner = (x - far) % 8 if way == 0 else (x + far) % 8
        push(
            piece(kind, owner),
            piece(kind, owner),
            send_sems.at[6 + kind],
            spread_sem.at[way, hop - 1, kind],
            at_x(chips if way == 0 else -chips),
        )

    def spread_own(kind):
        for way in range(2):
            if kind in SHORT_X:
                spread(kind, way, 2, 2)
            spread(kind, way, 1)

    def spread_hop(kind, hop):
        last_way = LAST_WAY_X[kind]
        for way in range(2):
            if hop == 4 and way != last_way:
                continue
            owner = (x - hop) % 8 if way == 0 else (x + hop) % 8
            wait(piece(kind, owner), spread_sem.at[way, hop - 1, kind])
            if kind in SHORT_X:
                if hop == 2:
                    if way == last_way:
                        spread(kind, way, 4, 2)
                    spread(kind, way, 3)
            elif hop < 3 or (hop == 3 and way == last_way):
                spread(kind, way, hop + 1)

    def gram_chunk(a):
        whole.settle(a)
        product = lax.dot_general(
            u_all[0:ROWS, :],
            u_all[CHUNK * a : CHUNK * a + CHUNK, :],
            (((1,), (1,)), ((), ())),
            preferred_element_type=F32,
        )
        stage[a] = product.astype(BF16).reshape(10, 16, CHUNK)
        for by in FARTHEST_FIRST:
            push(
                stage.at[a, (x + by) % 8],
                got.at[a, by],
                send_sems.at[5],
                got_sem.at[a],
                at_x(by),
            )
        for half in range(2):
            owner = 2 * a + half

            @pl.when(x != owner)
            def _():
                push(
                    stage.at[a, 8 + half],
                    got_rest.at[(owner - x) % 8],
                    send_sems.at[5],
                    rest_sem,
                    (f, owner),
                )

    for by in NEAREST_FIRST:
        push(message.at[(y + by) % 8], arrived.at[by], send_sems.at[0], owner_sem.at[by], at_y(by))
    arrived[0] = message[y]
    u_all[0:16, :] = arrived[0, :, :COLS]
    whole.send_own(0)

    def take(first, last):
        for p in range(first, last):
            d = ORDER[p]
            wait(arrived.at[d], owner_sem.at[d])
            u_all[16 * p : 16 * p + 16, :] = arrived[d, :, :COLS]

    take(1, 3)
    whole.send_own(1)
    take(3, 5)
    whole.send_own(2)
    take(5, 8)
    whole.send_own(3)
    packed = arrived[:, :, COLS:].reshape(128, 128)
    for k in range(4):
        chosen = selection((32, 128), lambda r: 16 * (r // 4) + 4 * k + r % 4)
        u_all[128:160, 128 * k : 128 * k + 128] = pick(chosen, packed).astype(BF16)
    whole.send_own(4)
    for hop in range(1, 5):
        for sub in range(SUBS):
            whole.step(hop, sub)
        gram_chunk(hop - 1)
        if hop == 3:
            reduce_chunk(0)
            reduce_chunk(1)
            spread_own(0)

    spread_hop(0, 1)
    reduce_chunk(2)
    spread_own(1)
    spread_hop(0, 2)
    reduce_chunk(3)
    spread_own(2)

    def image_of(sub):
        parts = [
            pl.ds(start if isinstance(start, int) else pl.multiple_of(start, 16), size)
            for start, size in images.parts[sub]
        ]
        total = None
        for a in range(CHUNKS):
            left = jnp.concatenate([gram[a, part, :] for part in parts], axis=0)
            product = jnp.dot(
                left, u_all[CHUNK * a : CHUNK * a + CHUNK, :], preferred_element_type=F32
            )
            total = product if total is None else total + product
        total, done = total.astype(BF16), 0
        for part in parts:
            v_all[part, :] = total[done : done + part.size]
            done += part.size
        images.send_own(sub)

    wait(got_rest.at[pl.ds(1, 7)], rest_sem)
    total = stage[x // 2, 8 + x % 2].astype(F32)
    for by in range(1, 8):
        total += got_rest[by].astype(F32)
    gram[x // 2, pl.ds(pl.multiple_of(128 + 16 * (x % 2), 16), 16), :] = total.astype(BF16)
    spread_own(3)
    image_of(0)

    def image_chunk(a):
        images.settle(a)
        product = jnp.dot(
            gram[a], v_all[CHUNK * a : CHUNK * a + CHUNK, :], preferred_element_type=F32
        )
        if a == 0:
            w_acc[...] = product
        else:
            w_acc[...] += product

    for turn in range(1, 9):
        if turn < 5:
            spread_hop(1, turn)
            spread_hop(2, turn)
            if turn in (2, 4):
                spread_hop(3, turn)
            image_of(turn)
            if turn in (1, 3):
                spread_hop(3, turn)
            if turn < 3:
                spread_hop(0, turn + 2)
        if turn == 4:
            sums = jnp.zeros((8, 128), F32)
            for b in range(CHUNKS):
                values = gram[b].astype(F32)
                part = jnp.sum((values * values).reshape(20, 8, CHUNK), axis=0)
                for k in range(CHUNK // 128):
                    sums += part[:, 128 * k : 128 * k + 128]
            squares[0] = sums
            push(squares.at[0], squares.at[1], send_sems.at[10], square_sem.at[0], sibling)
        if turn == 5:
            wait(squares.at[1], square_sem.at[0])
            squares[2] = squares[0] + squares[1]
            for by in range(1, 8):
                push(squares.at[2], squares.at[2 + by], send_sems.at[11], square_sem.at[1], at_z(by))
        for hop in range(1, 5):
            if 0 <= turn - hop < SUBS:
                images.step(hop, turn - hop)
        if turn >= 5:
            image_chunk(turn - 5)

    wait(squares.at[pl.ds(3, 7)], square_sem.at[1])
    total = squares[2]
    for by in range(1, 8):
        total += squares[2 + by]
    square_sum = jnp.sum(total, keepdims=True)
    factor = lax.rsqrt(jnp.sqrt(square_sum / H + tiny_value))
    factor_2 = factor * factor
    result = (math.sqrt(D) * factor) * (
        first_coef * u_all[0:ROWS, :].astype(F32)
        + (third_coef * factor_2) * v_all[0:ROWS, :].astype(F32)
        + (fifth_coef * factor_2 * factor_2) * w_acc[...]
    )
    result = result.astype(BF16)
    for p in range(8):
        reply[ORDER[p], :, :COLS] = result[16 * p : 16 * p + 16, :]
    rest = jnp.zeros((128, 128), F32)
    for k in range(4):
        chosen = selection(
            (128, 32), lambda r: jnp.where(r % 16 // 4 == k, 4 * (r // 16) + r % 4, -1)
        )
        rest += pick(chosen, result[128:160, 128 * k : 128 * k + 128])
    reply[:, :, COLS:] = rest.astype(BF16).reshape(8, 16, 128)
    for by in FARTHEST_FIRST:
        push(reply.at[by], returned.at[y], send_sems.at[12], return_sem, at_y(-by))
    returned[y] = reply[0]
    wait(returned.at[pl.ds(0, 7)], return_sem)
    main = returned[:, :, :COLS].reshape(128, COLS)
    main = pick(selection((128, 128), lambda r: 16 * (r % 8) + r // 8), main)
    out_ref[0:16] = main.reshape(16, 8, COLS).astype(BF16)
    rest = returned[:, :, COLS:].reshape(128, 128)
    for k in range(4):
        chosen = selection((32, 128), lambda r: 16 * (r % 8) + 4 * k + r // 8)
        out_ref[16:20, :, 128 * k : 128 * k + 128] = (
            pick(chosen, rest).reshape(4, 8, 128).astype(BF16)
        )

    wait(arrived.at[pl.ds(1, 7)], send_sems.at[0])
    wait(u_all.at[pl.ds(0, 7 * ROWS)], send_sems.at[1])
    wait(u_all.at[pl.ds(0, 8 * ROWS)], send_sems.at[2])
    wait(v_all.at[pl.ds(0, 7 * ROWS)], send_sems.at[3])
    wait(v_all.at[pl.ds(0, 8 * ROWS)], send_sems.at[4])
    for a in range(CHUNKS):
        wait(got.at[a, pl.ds(1, 7)], send_sems.at[5])
    wait(got_rest.at[pl.ds(1, 7)], send_sems.at[5])
    for kind in range(4):
        for _ in range(7):
            wait(piece(kind, x), send_sems.at[6 + kind])
    wait(squares.at[0], send_sems.at[10])
    wait(squares.at[pl.ds(3, 7)], send_sems.at[11])
    wait(reply.at[pl.ds(1, 7)], send_sems.at[12])


def step(gradient, momentum, row_counts):
    DMA = pltpu.SemaphoreType.DMA
    return pl.pallas_call(
        kernel,
        out_shape=jax.ShapeDtypeStruct((20, 8, COLS), BF16),
        in_specs=[pl.BlockSpec(memory_space=pl.ANY)] * 3,
        out_specs=pl.BlockSpec(memory_space=pltpu.VMEM),
        scratch_shapes=[
            pltpu.VMEM((20, 8, COLS), BF16),
            pltpu.VMEM((20, 8, COLS), F32),
            pltpu.VMEM((8, 128), jnp.int32),
            pltpu.VMEM((8, 16, WIDE), BF16),
            pltpu.VMEM((8, 16, WIDE), BF16),
            pltpu.VMEM((FULL, COLS), BF16),
            pltpu.VMEM((FULL, COLS), BF16),
            pltpu.VMEM((CHUNKS, 10, 16, CHUNK), BF16),
            pltpu.VMEM((CHUNKS, 8, 16, CHUNK), BF16),
            pltpu.VMEM((8, 16, CHUNK), BF16),
            pltpu.VMEM((CHUNKS, ROWS, CHUNK), BF16),
            pltpu.VMEM((ROWS, COLS), F32),
            pltpu.VMEM((10, 8, 128), F32),
            pltpu.VMEM((8, 16, WIDE), BF16),
            pltpu.VMEM((8, 16, WIDE), BF16),
            DMA((3,)),
            DMA((13,)),
            DMA((8,)),
            DMA((2, 4, SUBS)),
            DMA((8,)),
            DMA((2, 4, SUBS)),
            DMA((8,)),
            DMA((CHUNKS,)),
            DMA,
            DMA((2, 4, 4)),
            DMA((2,)),
            DMA,
        ],
        compiler_params=pltpu.CompilerParams(
            collective_id=0, has_side_effects=True, vmem_limit_bytes=63 * 1024 * 1024
        ),
    )(gradient, momentum, row_counts)


def finish(result_ref, gradient_ref, momentum_ref, new_ref, update_ref):
    new_ref[...] = keep_rate * momentum_ref[...] + gradient_ref[...].astype(F32)
    update_ref[...] = result_ref[...].astype(F32)


def on_device(gradient, momentum, row_counts):
    gradient, momentum = gradient.transpose(1, 0, 2), momentum.transpose(1, 0, 2)
    result = step(gradient, momentum, row_counts)
    new_momentum, update = pl.pallas_call(
        finish, out_shape=(jax.ShapeDtypeStruct(momentum.shape, F32),) * 2
    )(result, gradient, momentum)
    return (new_momentum.transpose(1, 0, 2), update.transpose(1, 0, 2))


def solution(mesh):
    placed = (P(None, "fsdp", "grp"), P(None, "fsdp", "grp"), P())
    return jax.shard_map(
        on_device,
        mesh=mesh,
        in_specs=placed,
        out_specs=(P(None, "fsdp", "grp"), P(None, "fsdp", "grp")),
        check_vma=False,
    )
```
